32 devices in a mesh: lon: 8 (over y, x, core), lat: 4 (over z).
Axes of the slice: x: 2, y: 2, z: 4, core: 2. Of those that a mesh axis runs over, the one named last changes fastest.
Arguments:
- cells: bfloat16 [256, 512, 128], P('lat', 'lon'), may hold values from -6 to 6
- ocean_mask: int32 [256, 512], P('lat', 'lon'), may hold values from 0 to 1, as said below
- cotangent: bfloat16 [256, 512, 128], P('lat', 'lon'), may hold values from -6 to 6
- kernel: float32 [7, 7, 128], replicated, may hold values from -0.875 to 0.875
- conv_bias: float32 [128], replicated, may hold values from -3 to 3
- gain: float32 [128], replicated, may hold values from 0.1 to 1.9
- shift: float32 [128], replicated, may hold values from -3 to 3
- w_in: bfloat16 [128, 512], replicated, may hold values from -0.5 to 0.5
- b_in: float32 [512], replicated, may hold values from -3 to 3
- w_out: bfloat16 [512, 128], replicated, may hold values from -0.25 to 0.25
Outputs:
- cells_grad: bfloat16 [256, 512, 128], P('lat', 'lon')
- grad_kernel: float32 [7, 7, 128], replicated
- grad_bias: float32 [128], replicated
- grad_gain: float32 [128], replicated
- grad_shift: float32 [128], replicated
- grad_in: float32 [128, 512], replicated
- grad_b: float32 [512], replicated
- grad_out: float32 [512, 128], replicated
The draws below stay inside these ranges and needn't reach their ends.
Inputs may be any that keep to these rules, and one draw needn't show every extreme that they name: `ocean_mask`: within each aligned 64 x 64 block the ocean cells are either all cells, none, or those on one side of a straight line; some blocks are all land and some all ocean.
All inputs are finite; a program needn't handle non-finite values.
Results may differ from the reference program's by a relative error of at most 0.006.
Values may be sent and summed in bfloat16 or wider, within the bound.
A program may use at most 128 MiB of HBM per device.

```python
import jax
import jax.numpy as jnp
from jax import lax

BS = 64
C = 128
HID = 512
KS = 7
HALF = 3
LATC = 256
LONC = 512


def draw_ocean_mask(key, part):
    rows_b = LATC // BS
    cols_b = LONC // BS
    key_kind, key_first, key_second, key_offset = jax.random.split(key, 4)
    kinds = jax.random.randint(key_kind, (rows_b, cols_b), 0, 4)
    eastern = (jnp.arange(cols_b, dtype=jnp.int32) >= cols_b // 2)[None, :]
    kinds = jnp.where(eastern & (kinds == 0), 1, kinds)
    kinds = kinds.at[0, 0].set(0).at[0, 1].set(1).at[0, cols_b // 2].set(1)
    slope_row = jax.random.randint(key_first, (rows_b, cols_b), -3, 4)
    slope_col = jax.random.randint(key_second, (rows_b, cols_b), -3, 4)
    offsets = jax.random.randint(key_offset, (rows_b, cols_b), -2 * BS, 2 * BS)

    def expand(table):
        return jnp.repeat(jnp.repeat(table, BS, axis=0), BS, axis=1)
    local_row = (jnp.arange(LATC, dtype=jnp.int32) % BS - BS // 2)[:, None]
    local_col = (jnp.arange(LONC, dtype=jnp.int32) % BS - BS // 2)[None, :]
    coast = (expand(slope_row) * local_row + expand(slope_col) * local_col > expand(offsets)).astype(jnp.int32)
    kind_cells = expand(kinds)
    return jnp.where(kind_cells == 0, 0, jnp.where(kind_cells == 1, 1, coast)).astype(jnp.int32)


def steps_of(stream_key, shape, pieces, least, high):
    factor_of, own = 1.0, jax.random.fold_in(stream_key, 6)
    for position, shards_of in pieces:
        steps = jnp.exp(jax.random.uniform(jax.random.fold_in(own, position), (shards_of,), jnp.float32, least / len(pieces), high / len(pieces)))
        factor_of = factor_of * jnp.repeat(steps, shape[position] // shards_of).reshape([-1 if axis == position else 1 for axis in range(len(shape))])
    return factor_of


def scatter_about(key, shape, width, most, pieces=(), kind=jnp.bfloat16):
    values = jax.random.normal(key, shape, jnp.float32) * width
    if len(pieces) > 0:
        values = steps_of(key, shape, pieces, -0.22, 0.18) * values
    return jnp.clip(values, min=-most, max=most).astype(kind)


def setup_inputs(seed: int = 0) -> dict:
    splits = jax.random.split(jax.random.key(seed), 11)
    cells = scatter_about(splits[0], (LATC, LONC, C), 1.0, 6.0, ((0, 4), (1, 8)))
    ocean_mask = draw_ocean_mask(jax.random.fold_in(splits[10], 71), 0)
    cotangent = scatter_about(splits[2], (LATC, LONC, C), 1.0, 6.0, ((0, 4), (1, 8)))
    kernel = scatter_about(splits[3], (KS, KS, C), (KS * KS) ** -0.5, 0.875, (), jnp.float32)
    conv_bias = scatter_about(splits[4], (C,), 0.5, 3.0, (), jnp.float32)
    gain = jnp.clip(1.0 + 0.18 * jax.random.normal(splits[5], (C,), jnp.float32), 0.1, 1.9)
    shift = scatter_about(splits[6], (C,), 0.5, 3.0, (), jnp.float32)
    w_in = scatter_about(splits[7], (C, HID), C ** -0.5, 0.5)
    b_in = scatter_about(splits[8], (HID,), 0.5, 3.0, (), jnp.float32)
    w_out = scatter_about(splits[9], (HID, C), HID ** -0.5, 0.25)
    return dict(cells=cells, ocean_mask=ocean_mask, cotangent=cotangent, kernel=kernel, conv_bias=conv_bias, gain=gain, shift=shift, w_in=w_in, b_in=b_in, w_out=w_out)


def depthwise(padded, kernel, height, across):
    summed = jnp.zeros((height, across, padded.shape[2]), jnp.float32)
    for row_off in range(KS):
        for col_off in range(KS):
            summed = summed + kernel[row_off, col_off] * padded[row_off:row_off + height, col_off:col_off + across].astype(jnp.float32)
    return summed

def transposed(padded, kernel, height, across):
    summed = jnp.zeros((height, across, padded.shape[2]), jnp.float32)
    for row_off in range(KS):
        for col_off in range(KS):
            first_row = KS - 1 - row_off
            first_col = KS - 1 - col_off
            summed = summed + kernel[row_off, col_off] * padded[first_row:first_row + height, first_col:first_col + across].astype(jnp.float32)
    return summed

def gelu_tanh(value):
    return jax.nn.gelu(value, approximate=True)

def forward_part(padded, ocean, cotangent, kernel, conv_bias, gain, shift, w_in, b_in, w_out):
    height, across, channels = cotangent.shape
    conv = depthwise(padded, kernel, height, across) + conv_bias
    average = lax.optimization_barrier(jnp.mean(conv, axis=-1, keepdims=True))
    centred = conv - average
    variance = lax.optimization_barrier(jnp.mean(centred * centred, axis=-1, keepdims=True))
    inverse_std = lax.rsqrt(variance + 1e-06)
    scaled = centred * inverse_std
    normed = (scaled * gain + shift).astype(jnp.bfloat16).reshape(height * across, channels)
    preact = jnp.dot(normed, w_in, preferred_element_type=jnp.float32) + b_in
    activation = gelu_tanh(preact).astype(jnp.bfloat16)
    out_grad = (cotangent * ocean).reshape(height * across, channels)
    grad_out = lax.dot_general(activation, out_grad, (((0,), (0,)), ((), ())), preferred_element_type=jnp.float32)
    act_grad = lax.dot_general(out_grad, w_out, (((1,), (1,)), ((), ())), preferred_element_type=jnp.float32)
    hidden_grad = jax.vjp(gelu_tanh, preact)[1](act_grad)[0].astype(jnp.bfloat16)
    return (normed, scaled, inverse_std, hidden_grad, grad_out)

def backward_part(padded, normed, scaled, inverse_std, hidden_grad, gain, w_in):
    height, across, channels = scaled.shape
    grad_in = lax.dot_general(normed, hidden_grad, (((0,), (0,)), ((), ())), preferred_element_type=jnp.float32)
    grad_b = lax.optimization_barrier(jnp.sum(hidden_grad.astype(jnp.float32), axis=0))
    norm_grad = lax.dot_general(hidden_grad, w_in, (((1,), (1,)), ((), ())), preferred_element_type=jnp.float32).reshape(height, across, channels)
    grad_gain = lax.optimization_barrier(jnp.sum(norm_grad * scaled, axis=(0, 1)))
    grad_shift = lax.optimization_barrier(jnp.sum(norm_grad, axis=(0, 1)))
    weighted = norm_grad * gain
    conv_grad = (inverse_std * (weighted - lax.optimization_barrier(jnp.mean(weighted, axis=-1, keepdims=True)) - scaled * lax.optimization_barrier(jnp.mean(weighted * scaled, axis=-1, keepdims=True)))).astype(jnp.bfloat16)
    conv_wide = conv_grad.astype(jnp.float32)
    grad_bias = lax.optimization_barrier(jnp.sum(conv_wide, axis=(0, 1)))
    rows_list = []
    for row_off in range(KS):
        cols_list = []
        for col_off in range(KS):
            window = padded[row_off:row_off + height, col_off:col_off + across].astype(jnp.float32)
            cols_list.append(lax.optimization_barrier(jnp.sum(conv_wide * window, axis=(0, 1))))
        rows_list.append(jnp.stack(cols_list))
    grad_kernel = jnp.stack(rows_list)
    return (conv_grad, grad_kernel, grad_bias, grad_gain, grad_shift, grad_in, grad_b)

def pad_grid(field):
    wrapped = jnp.concatenate([field[:, -HALF:], field, field[:, :HALF]], axis=1)
    return jnp.pad(wrapped, ((HALF, HALF), (0, 0), (0, 0)))

def reference(cells, ocean_mask, cotangent, kernel, conv_bias, gain, shift, w_in, b_in, w_out):
    ocean = ocean_mask.astype(jnp.bfloat16)[..., None]
    masked = cells * ocean
    padded = pad_grid(masked)
    slabs = LATC // BS

    def one_slab(running, slab):
        first_row = slab * BS
        window = lax.dynamic_slice_in_dim(padded, first_row, BS + 2 * HALF, 0)
        cot_slab = lax.dynamic_slice_in_dim(cotangent, first_row, BS, 0)
        ocean_slab = lax.dynamic_slice_in_dim(ocean, first_row, BS, 0)
        normed, scaled, inverse_std, hidden_grad, grad_out = forward_part(window, ocean_slab, cot_slab, kernel, conv_bias, gain, shift, w_in, b_in, w_out)
        results = backward_part(window, normed, scaled, inverse_std, hidden_grad, gain, w_in)
        partial_value = tuple(results[1:]) + (grad_out,)
        return (jax.tree.map(lambda left, right: left + right, running, partial_value), results[0])
    start = (jnp.zeros((KS, KS, C), jnp.float32), jnp.zeros((C,), jnp.float32), jnp.zeros((C,), jnp.float32), jnp.zeros((C,), jnp.float32), jnp.zeros((C, HID), jnp.float32), jnp.zeros((HID,), jnp.float32), jnp.zeros((HID, C), jnp.float32))
    totals, conv_grads = lax.scan(one_slab, start, jnp.arange(slabs, dtype=jnp.int32))
    conv_grad = conv_grads.reshape(LATC, LONC, C)
    grad_padded = pad_grid(conv_grad)

    def back_slab(slab):
        first_row = slab * BS
        window = lax.dynamic_slice_in_dim(grad_padded, first_row, BS + 2 * HALF, 0)
        cot_slab = lax.dynamic_slice_in_dim(cotangent, first_row, BS, 0)
        ocean_slab = lax.dynamic_slice_in_dim(ocean, first_row, BS, 0)
        spread_back = transposed(window, kernel, BS, LONC)
        return ((cot_slab.astype(jnp.float32) + spread_back) * ocean_slab.astype(jnp.float32)).astype(jnp.bfloat16)
    cells_grad = lax.map(back_slab, jnp.arange(slabs, dtype=jnp.int32)).reshape(LATC, LONC, C)
    factor = lax.rsqrt(jnp.float32(LATC * LONC))
    grad_kernel, grad_bias, grad_gain, grad_shift, grad_in, grad_b, grad_out = [entry * factor for entry in totals]
    return (cells_grad, grad_kernel, grad_bias, grad_gain, grad_shift, grad_in, grad_b, grad_out)
```

```python
import functools
import math

import jax
import jax.numpy as jnp
from jax import lax
from jax.experimental import pallas as pl
from jax.experimental.pallas import tpu as pltpu
from jax.sharding import PartitionSpec as P

KS = 7
HALF = 3
BS = 64
C = 128
HID = 512
LEFT = 8
WIDE = 80
TALL = BS + 2 * HALF
PAIRS = TALL // 2
BIG = 2 * HID
SMALL = 64
MESH = pl.DeviceIdType.MESH
F32 = jnp.float32
BF16 = jnp.bfloat16
MOVES = ((0, 1), (0, -1), (1, 0), (-1, 0), (1, 1), (1, -1), (-1, 1), (-1, -1))


def mm(a, b, dims=((1,), (0,))):
    return lax.dot_general(a, b, (dims, ((), ())), preferred_element_type=F32)


def plan(n_lon, n_lat):
    part = -(-BIG // (n_lon * n_lat * 16)) * 16
    small = max(SMALL // n_lon, 8)
    return part, small


def block_kernel(
    n_lon, n_lat,
    cells, mask, cot, kern, bias, gain, shift, w_in, b_in, w_out,
    o_cells, o_kernel, o_bias, o_gain, o_shift, o_in, o_b, o_out,
    padf, gradf, padp, gradp, w_fwd, w_bwd, convb, grad_t, maskx, acc_in, acc_out, vecs,
    h_send, h_recv, c_recv,
    big, big_lon, big_lat, big_sum, big_all, small, small_lon, small_lat, small_sum, small_all,
    hs_sem, hr_sem, s_sem, r_sem,
):
    part, small_part = plan(n_lon, n_lat)
    strip = n_lat * part
    lon = lax.axis_index("lon")
    lat = lax.axis_index("lat")
    lons = [lax.rem(lon + d, n_lon) for d in range(1, n_lon)]
    lats = [lax.rem(lat + d, n_lat) for d in range(1, n_lat)]

    def dev(a, b):
        return {"lat": a, "lon": b}

    def step_lon(d):
        return lax.rem(lon + d + n_lon, n_lon)

    def has(d):
        return (lat > 0) if d < 0 else (lat < n_lat - 1)

    barrier = pltpu.get_barrier_semaphore()
    for other in lons:
        pl.semaphore_signal(barrier, inc=1, device_id=dev(lat, other), device_id_type=MESH)
    for other in lats:
        pl.semaphore_signal(barrier, inc=1, device_id=dev(other, lon), device_id_type=MESH)
    for dlat, dlon in MOVES[4:]:
        corner = dev(lax.rem(lat + dlat + n_lat, n_lat), step_lon(dlon))
        pl.semaphore_signal(barrier, inc=1, device_id=corner, device_id_type=MESH)

    mask_t = mask[...].astype(F32).T
    padf3 = padf.reshape(TALL, WIDE, C)
    gradf3 = gradf.reshape(TALL, WIDE, C)
    for field in (padf3, gradf3):
        field[0:HALF] = jnp.zeros((HALF, WIDE, C), F32)
        field[BS + HALF : TALL] = jnp.zeros((HALF, WIDE, C), F32)
    for row in range(BS):
        spread = jnp.broadcast_to(mask_t[:, row : row + 1], (BS, C))
        maskx[row] = spread.astype(BF16)
        padf3[HALF + row, LEFT : LEFT + BS, :] = cells[row].astype(F32) * spread

    pl.semaphore_wait(barrier, n_lon + n_lat + 2)

    def halo_copy(turn, move):
        dlat, dlon = MOVES[move]
        if move < 4:
            src, dst = h_send.at[turn, move], h_recv.at[turn, move]
        else:
            src = h_send.at[turn, 2 if dlat > 0 else 3, :, pl.ds(48 if dlon > 0 else 0, 16), :]
            dst = c_recv.at[turn, move - 4]
        return pltpu.make_async_remote_copy(
            src_ref=src, dst_ref=dst,
            send_sem=hs_sem.at[turn, move], recv_sem=hr_sem.at[turn, move],
            device_id=dev(lat + dlat, step_lon(dlon)), device_id_type=MESH,
        )

    def halo_send(turn, field, field3):
        for k in range(HALF):
            last = field[pl.ds(HALF * WIDE + LEFT + BS - HALF + k, BS, stride=WIDE), :]
            first = field[pl.ds(HALF * WIDE + LEFT + k, BS, stride=WIDE), :]
            h_send[turn, 0, k] = last.astype(BF16)
            h_send[turn, 1, k] = first.astype(BF16)
            h_send[turn, 2, k] = field3[BS + k, LEFT : LEFT + BS, :].astype(BF16)
            h_send[turn, 3, k] = field3[HALF + k, LEFT : LEFT + BS, :].astype(BF16)
        for move, (dlat, _) in enumerate(MOVES):
            if dlat == 0:
                halo_copy(turn, move).start()
            else:
                @pl.when(has(dlat))
                def _(move=move):
                    halo_copy(turn, move).start()

    def halo_wait(turn, field, field3):
        for move, (dlat, dlon) in enumerate(MOVES):
            if dlat == 0:
                halo_copy(turn, move).wait()
                at = LEFT - HALF if dlon > 0 else LEFT + BS
                for k in range(HALF):
                    field[pl.ds(HALF * WIDE + at + k, BS, stride=WIDE), :] = h_recv[
                        turn, move, k
                    ].astype(F32)
            else:
                @pl.when(has(dlat))
                def _(move=move):
                    halo_copy(turn, move).wait_send()

                @pl.when(has(-dlat))
                def _(move=move, dlat=dlat, dlon=dlon):
                    halo_copy(turn, move).wait_recv()
                    at = 0 if dlat > 0 else BS + HALF
                    if move < 4:
                        field3[at : at + HALF, LEFT : LEFT + BS, :] = h_recv[turn, move].astype(F32)
                    else:
                        got = c_recv[turn, move - 4].astype(F32)
                        if dlon > 0:
                            field3[at : at + HALF, 0:LEFT, :] = got[:, 8:16, :]
                        else:
                            field3[at : at + HALF, LEFT + BS : WIDE, :] = got[:, 0:8, :]

    def spread_pairs(field3, pairs):
        def one(r, carry):
            for b in range(KS):
                for h in range(2):
                    pairs[b, r, :, h * C : (h + 1) * C] = field3[
                        2 * r + h, pl.ds(LEFT - HALF + b, BS), :
                    ].astype(BF16)
            return carry
        lax.fori_loop(0, PAIRS, one, 0)

    def conv_chunk(pairs, weights, t):
        taps = [
            pairs[b, pl.ds(8 * t + q, 8)].reshape(8 * BS, 2 * C) for b in range(KS) for q in range(4)
        ]
        return mm(jnp.concatenate(taps, axis=1), weights[...])

    halo_send(0, padf, padf3)

    eye = lax.broadcasted_iota(jnp.int32, (C, C), 0) == lax.broadcasted_iota(jnp.int32, (C, C), 1)
    none = jnp.zeros((C, C), BF16)
    for weights, flip in ((w_fwd, False), (w_bwd, True)):
        for b in range(KS):
            taps = []
            for a in range(KS):
                row = kern[KS - 1 - a, KS - 1 - b] if flip else kern[a, b]
                taps.append(jnp.where(eye, row[None, :], 0.0).astype(BF16))
            taps = [none] + taps + [none]
            for q in range(4):
                at = (b * 4 + q) * 2 * C
                weights[at : at + C, 0:C] = taps[2 * q + 1]
                weights[at : at + C, C : 2 * C] = taps[2 * q]
                weights[at + C : at + 2 * C, 0:C] = taps[2 * q + 2]
                weights[at + C : at + 2 * C, C : 2 * C] = taps[2 * q + 1]

    acc_in[...] = jnp.zeros_like(acc_in)
    acc_out[...] = jnp.zeros_like(acc_out)
    vecs[...] = jnp.zeros_like(vecs)
    halo_wait(0, padf, padf3)
    spread_pairs(padf3, padp)

    def forward(t, carry):
        convb[pl.ds(t * 512, 512), :] = conv_chunk(padp, w_fwd, t)
        return carry
    lax.fori_loop(0, 4, forward, 0)

    c1 = math.sqrt(2.0 / math.pi)
    c2 = c1 * 0.044715
    order = (0, 2, 4, 6, 1, 3, 5, 7)

    def cell_chunk(t, carry):
        two = convb[pl.ds(pl.multiple_of(t * 256, 256), 256), :]
        conv = jnp.concatenate([two[:, :C], two[:, C:]], axis=0) + bias[...]
        centred = conv - jnp.mean(conv, axis=-1, keepdims=True)
        inverse_std = lax.rsqrt(jnp.mean(centred * centred, axis=-1, keepdims=True) + 1e-06)
        scaled = centred * inverse_std
        normed = (scaled * gain[...] + shift[...]).astype(BF16)
        og = jnp.concatenate([cot[8 * t + i] * maskx[8 * t + i] for i in order], axis=0)
        normed_t = normed.T
        og_t = og.T
        ones = jnp.ones((16, 512), BF16)
        left = jnp.concatenate([normed_t, ones], axis=0)
        norm_grad = jnp.zeros((512, C), F32)
        for h in range(2):
            cols = slice(h * 256, (h + 1) * 256)
            v = mm(normed, w_in[:, cols]) + b_in[:, cols]
            act_grad = mm(og, w_out[cols, :], ((1,), (1,)))
            v2 = v * v
            t_half = 0.5 + 0.5 * jnp.tanh(v * (c1 + c2 * v2))
            act = v * t_half
            slope = t_half + act * (1.0 - t_half) * (2.0 * c1 + 6.0 * c2 * v2)
            hidden = (act_grad * slope).astype(BF16)
            acc_out[:, cols] += mm(og_t, act.astype(BF16))
            acc_in[:, cols] += mm(left, hidden)
            norm_grad += mm(hidden, w_in[:, cols], ((1,), (1,)))
        weighted = norm_grad * gain[...]
        product = norm_grad * scaled
        g = inverse_std * (
            weighted
            - jnp.mean(weighted, axis=-1, keepdims=True)
            - scaled * jnp.mean(weighted * scaled, axis=-1, keepdims=True)
        )
        g = g.astype(BF16)
        wide = g.astype(F32)
        vecs[0] += wide.reshape(64, 8, C).sum(0)
        vecs[1] += product.reshape(64, 8, C).sum(0)
        vecs[2] += norm_grad.reshape(64, 8, C).sum(0)
        grad_t[:, pl.ds(pl.multiple_of(t * 256, 256), 256)] = jnp.concatenate(
            [g[:256], g[256:]], axis=1
        ).T
        for n, i in enumerate(order):
            gradf3[HALF + 8 * t + i, LEFT : LEFT + BS, :] = wide[n * BS : (n + 1) * BS]
        return carry
    lax.fori_loop(0, 8, cell_chunk, 0)

    halo_send(1, gradf, gradf3)

    if big.shape[0] > BIG:
        big[BIG:, :] = jnp.zeros((big.shape[0] - BIG, C), F32)
    for h in range(4):
        big[h * C : (h + 1) * C, :] = acc_in[0:C, h * C : (h + 1) * C]
        big[HID + h * C : HID + (h + 1) * C, :] = acc_out[:, h * C : (h + 1) * C].T

    def copy(src, dst, group, mine, other, to):
        return pltpu.make_async_remote_copy(
            src_ref=src, dst_ref=dst.at[mine], send_sem=s_sem.at[group, other],
            recv_sem=r_sem.at[group, mine], device_id=to, device_id_type=MESH,
        )

    def arrived(dst, group, other, to):
        pltpu.make_async_remote_copy(
            src_ref=dst.at[other], dst_ref=dst.at[other], send_sem=s_sem.at[group, other],
            recv_sem=r_sem.at[group, other], device_id=to, device_id_type=MESH,
        ).wait_recv()

    def send_parts(src, rows, dst, group):
        for other in lons:
            at = pl.multiple_of(other * rows, 8)
            copy(src.at[pl.ds(at, rows)], dst, group, lon, other, dev(lat, other)).start()
        dst[lon] = src[pl.ds(pl.multiple_of(lon * rows, 8), rows), :]

    def end(src, rows, dst, group, peers, along):
        for other in peers:
            to = dev(lat, other) if along == "lon" else dev(other, lon)
            mine = lon if along == "lon" else lat
            copy(src.at[pl.ds(0, rows)], dst, group, mine, other, to).wait_send()
            arrived(dst, group, other, to)

    def total(slots, count):
        out = slots[0]
        for k in range(1, count):
            out = out + slots[k]
        return out

    send_parts(big, strip, big_lon, 0)

    def kernel_column(b, carry):
        rows = [jnp.zeros((1, C), F32) for _ in range(KS + 2)]
        for q in range(4):
            both = mm(grad_t[...], padp[b, q : q + 32].reshape(2048, 2 * C))

            def diagonal(e, s):
                block = both[e * C : (e + 1) * C, s * C : (s + 1) * C]
                return jnp.sum(jnp.where(eye, block, 0.0), axis=0, keepdims=True)
            rows[2 * q + 1] = rows[2 * q + 1] + diagonal(0, 0) + diagonal(1, 1)
            if q < 3:
                rows[2 * q + 2] = rows[2 * q + 2] + diagonal(0, 1)
            if q > 0:
                rows[2 * q] = rows[2 * q] + diagonal(1, 0)
        small[pl.ds(pl.multiple_of(b * 8, 8), 8), :] = jnp.concatenate(
            rows[1:8] + [jnp.zeros((1, C), F32)], axis=0
        )
        return carry
    lax.fori_loop(0, KS, kernel_column, 0)

    if small.shape[0] > SMALL:
        small[SMALL:, :] = jnp.zeros((small.shape[0] - SMALL, C), F32)
    small[56:64, :] = jnp.concatenate(
        [jnp.sum(vecs[k], axis=0, keepdims=True) for k in range(3)]
        + [acc_in[C : C + 1, h * C : (h + 1) * C] for h in range(4)]
        + [jnp.zeros((1, C), F32)],
        axis=0,
    )
    send_parts(small, small_part, small_lon, 1)

    halo_wait(1, gradf, gradf3)
    spread_pairs(gradf3, gradp)

    def backward(t):
        two = conv_chunk(gradp, w_bwd, t)
        for i in range(8):
            for e in range(2):
                row = 16 * t + 2 * i + e
                back = two[i * BS : (i + 1) * BS, e * C : (e + 1) * C]
                o_cells[row] = ((cot[row].astype(F32) + back) * maskx[row].astype(F32)).astype(BF16)

    backward(0)
    end(big, strip, big_lon, 0, lons, "lon")
    end(small, small_part, small_lon, 1, lons, "lon")
    big_sum[...] = total(big_lon, n_lon)
    small_sum[...] = total(small_lon, n_lon)
    for other in lats:
        at = pl.multiple_of(other * part, 8)
        copy(big_sum.at[pl.ds(at, part)], big_lat, 2, lat, other, dev(other, lon)).start()
        copy(small_sum, small_lat, 3, lat, other, dev(other, lon)).start()
    big_lat[lat] = big_sum[pl.ds(pl.multiple_of(lat * part, 8), part), :]
    small_lat[lat] = small_sum[...]

    backward(1)
    end(big_sum, part, big_lat, 2, lats, "lat")
    end(small_sum, small_part, small_lat, 3, lats, "lat")
    factor = 1.0 / math.sqrt(float(BS * BS * n_lon * n_lat))
    own = pl.ds(pl.multiple_of(lat * part, 8), part)
    big_all[lon, own, :] = total(big_lat, n_lat) * factor
    small_all[lon] = total(small_lat, n_lat) * factor

    def spread_lat(other):
        return pltpu.make_async_remote_copy(
            src_ref=big_all.at[lon, own], dst_ref=big_all.at[lon, own],
            send_sem=s_sem.at[4, other], recv_sem=r_sem.at[4, lat],
            device_id=dev(other, lon), device_id_type=MESH,
        )

    for other in lats:
        spread_lat(other).start()
    for other in lons:
        copy(small_all.at[lon], small_all, 6, lon, other, dev(lat, other)).start()

    backward(2)
    for other in lats:
        spread_lat(other).wait_send()
        theirs = big_all.at[lon, pl.ds(pl.multiple_of(other * part, 8), part)]
        pltpu.make_async_remote_copy(
            src_ref=theirs, dst_ref=theirs, send_sem=s_sem.at[4, other],
            recv_sem=r_sem.at[4, other], device_id=dev(other, lon), device_id_type=MESH,
        ).wait_recv()
    for other in lons:
        copy(big_all.at[lon], big_all, 5, lon, other, dev(lat, other)).start()

    backward(3)
    for other in lons:
        copy(big_all.at[lon], big_all, 5, lon, other, dev(lat, other)).wait_send()
        arrived(big_all, 5, other, dev(lat, other))
        copy(small_all.at[lon], small_all, 6, lon, other, dev(lat, other)).wait_send()
        arrived(small_all, 6, other, dev(lat, other))

    flat = big_all.reshape(n_lon * strip, C)
    for h in range(4):
        o_in[:, h * C : (h + 1) * C] = flat[h * C : (h + 1) * C, :]
    o_out[...] = flat[HID : 2 * HID, :]
    rest = small_all.reshape(n_lon * small_part, C)
    for a in range(KS):
        for b in range(KS):
            o_kernel[a, b : b + 1, :] = rest[8 * b + a : 8 * b + a + 1, :]
    o_bias[...] = rest[56:57, :]
    o_gain[...] = rest[57:58, :]
    o_shift[...] = rest[58:59, :]
    for h in range(4):
        o_b[:, h * C : (h + 1) * C] = rest[59 + h : 60 + h, :]


def body(n_lon, n_lat, cells, ocean_mask, cotangent, kernel, conv_bias, gain, shift, w_in, b_in, w_out):
    part, small_part = plan(n_lon, n_lat)
    strip = n_lat * part
    vmem = pl.BlockSpec(memory_space=pltpu.VMEM)
    most = max(n_lon, n_lat)
    outs = pl.pallas_call(
        functools.partial(block_kernel, n_lon, n_lat),
        out_shape=(
            jax.ShapeDtypeStruct((BS, BS, C), BF16),
            jax.ShapeDtypeStruct((KS, KS, C), F32),
            jax.ShapeDtypeStruct((1, C), F32),
            jax.ShapeDtypeStruct((1, C), F32),
            jax.ShapeDtypeStruct((1, C), F32),
            jax.ShapeDtypeStruct((C, HID), F32),
            jax.ShapeDtypeStruct((1, HID), F32),
            jax.ShapeDtypeStruct((HID, C), F32),
        ),
        in_specs=[vmem] * 10,
        out_specs=(vmem,) * 8,
        scratch_shapes=[
            pltpu.VMEM((TALL * WIDE, C), F32),
            pltpu.VMEM((TALL * WIDE, C), F32),
            pltpu.VMEM((KS, PAIRS, BS, 2 * C), BF16),
            pltpu.VMEM((KS, PAIRS, BS, 2 * C), BF16),
            pltpu.VMEM((KS * 4 * 2 * C, 2 * C), BF16),
            pltpu.VMEM((KS * 4 * 2 * C, 2 * C), BF16),
            pltpu.VMEM((2048, 2 * C), F32),
            pltpu.VMEM((2 * C, 2048), BF16),
            pltpu.VMEM((BS, BS, C), BF16),
            pltpu.VMEM((C + 16, HID), F32),
            pltpu.VMEM((C, HID), F32),
            pltpu.VMEM((3, 8, C), F32),
            pltpu.VMEM((2, 4, HALF, BS, C), BF16),
            pltpu.VMEM((2, 4, HALF, BS, C), BF16),
            pltpu.VMEM((2, 4, HALF, 16, C), BF16),
            pltpu.VMEM((n_lon * strip, C), F32),
            pltpu.VMEM((n_lon, strip, C), F32),
            pltpu.VMEM((n_lat, part, C), F32),
            pltpu.VMEM((strip, C), F32),
            pltpu.VMEM((n_lon, strip, C), F32),
            pltpu.VMEM((n_lon * small_part, C), F32),
            pltpu.VMEM((n_lon, small_part, C), F32),
            pltpu.VMEM((n_lat, small_part, C), F32),
            pltpu.VMEM((small_part, C), F32),
            pltpu.VMEM((n_lon, small_part, C), F32),
            pltpu.SemaphoreType.DMA((2, 8)),
            pltpu.SemaphoreType.DMA((2, 8)),
            pltpu.SemaphoreType.DMA((7, most)),
            pltpu.SemaphoreType.DMA((7, most)),
        ],
        compiler_params=pltpu.CompilerParams(
            collective_id=0, has_side_effects=True, vmem_limit_bytes=56 * 2**20
        ),
    )(
        cells, ocean_mask, cotangent, kernel, conv_bias[None, :], gain[None, :], shift[None, :],
        w_in, b_in[None, :], w_out,
    )
    g_cells, g_kernel, g_bias, g_gain, g_shift, g_in, g_b, g_out = outs
    return (g_cells, g_kernel, g_bias[0], g_gain[0], g_shift[0], g_in, g_b[0], g_out)


def solution(mesh):
    grid = P("lat", "lon", None)
    in_specs = (grid, P("lat", "lon"), grid) + (P(),) * 7
    out_specs = (grid,) + (P(),) * 7
    return jax.shard_map(
        functools.partial(body, mesh.shape["lon"], mesh.shape["lat"]),
        mesh=mesh, in_specs=in_specs, out_specs=out_specs, check_vma=False,
    )
```

```python
import functools
import math

import jax
import jax.numpy as jnp
from jax import lax
from jax.experimental import pallas as pl
from jax.experimental.pallas import tpu as pltpu
from jax.sharding import PartitionSpec as P

KS = 7
HALF = 3
BS = 64
C = 128
HID = 512
LEFT = 8
WIDE = 80
TALL = BS + 2 * HALF
PAIRS = TALL // 2
BIG = 2 * HID
SMALL = 64
MESH = pl.DeviceIdType.MESH
F32 = jnp.float32
BF16 = jnp.bfloat16
MOVES = ((0, 1), (0, -1), (1, 0), (-1, 0), (1, 1), (1, -1), (-1, 1), (-1, -1))


def mm(a, b, dims=((1,), (0,))):
    return lax.dot_general(a, b, (dims, ((), ())), preferred_element_type=F32)


def plan(n_lon, n_lat):
    part = -(-BIG // (n_lon * n_lat * 16)) * 16
    small = max(SMALL // n_lon, 8)
    return part, small


def block_kernel(
    n_lon, n_lat,
    cells, mask, cot, kern, bias, gain, shift, w_in, b_in, w_out,
    o_cells, o_kernel, o_bias, o_gain, o_shift, o_in, o_b, o_out,
    padf, gradf, padp, gradp, w_fwd, w_bwd, convb, grad_t, maskx, acc_in, acc_out, vecs,
    h_send, h_recv, c_recv,
    big, big_lon, big_lat, big_sum, big_all, small, small_lon, small_lat, small_sum, small_all,
    hs_sem, hr_sem, s_sem, r_sem,
):
    part, small_part = plan(n_lon, n_lat)
    strip = n_lat * part
    lon = lax.axis_index("lon")
    lat = lax.axis_index("lat")
    lons = [lax.rem(lon + d, n_lon) for d in range(1, n_lon)]
    lats = [lax.rem(lat + d, n_lat) for d in range(1, n_lat)]

    def dev(a, b):
        return {"lat": a, "lon": b}

    def step_lon(d):
        return lax.rem(lon + d + n_lon, n_lon)

    def has(d):
        return (lat > 0) if d < 0 else (lat < n_lat - 1)

    barrier = pltpu.get_barrier_semaphore()
    for other in lons:
        pl.semaphore_signal(barrier, inc=1, device_id=dev(lat, other), device_id_type=MESH)
    for other in lats:
        pl.semaphore_signal(barrier, inc=1, device_id=dev(other, lon), device_id_type=MESH)
    for dlat, dlon in MOVES[4:]:
        corner = dev(lax.rem(lat + dlat + n_lat, n_lat), step_lon(dlon))
        pl.semaphore_signal(barrier, inc=1, device_id=corner, device_id_type=MESH)

    mask_t = mask[...].astype(F32).T
    padf3 = padf.reshape(TALL, WIDE, C)
    gradf3 = gradf.reshape(TALL, WIDE, C)
    for field in (padf3, gradf3):
        field[0:HALF] = jnp.zeros((HALF, WIDE, C), F32)
        field[BS + HALF : TALL] = jnp.zeros((HALF, WIDE, C), F32)
    for row in range(BS):
        spread = jnp.broadcast_to(mask_t[:, row : row + 1], (BS, C))
        maskx[row] = spread.astype(BF16)
        padf3[HALF + row, LEFT : LEFT + BS, :] = cells[row].astype(F32) * spread

    pl.semaphore_wait(barrier, n_lon + n_lat + 2)

    def halo_copy(turn, move):
        dlat, dlon = MOVES[move]
        if move < 4:
            src, dst = h_send.at[turn, move], h_recv.at[turn, move]
        else:
            src = h_send.at[turn, 2 if dlat > 0 else 3, :, pl.ds(48 if dlon > 0 else 0, 16), :]
            dst = c_recv.at[turn, move - 4]
        return pltpu.make_async_remote_copy(
            src_ref=src, dst_ref=dst,
            send_sem=hs_sem.at[turn, move], recv_sem=hr_sem.at[turn, move],
            device_id=dev(lat + dlat, step_lon(dlon)), device_id_type=MESH,
        )

    def halo_send(turn, field, field3):
        for k in range(HALF):
            last = field[pl.ds(HALF * WIDE + LEFT + BS - HALF + k, BS, stride=WIDE), :]
            first = field[pl.ds(HALF * WIDE + LEFT + k, BS, stride=WIDE), :]
            h_send[turn, 0, k] = last.astype(BF16)
            h_send[turn, 1, k] = first.astype(BF16)
            h_send[turn, 2, k] = field3[BS + k, LEFT : LEFT + BS, :].astype(BF16)
            h_send[turn, 3, k] = field3[HALF + k, LEFT : LEFT + BS, :].astype(BF16)
        for move, (dlat, _) in enumerate(MOVES):
            if dlat == 0:
                halo_copy(turn, move).start()
            else:
                @pl.when(has(dlat))
                def _(move=move):
                    halo_copy(turn, move).start()

    def halo_wait(turn, field, field3):
        for move, (dlat, dlon) in enumerate(MOVES):
            if dlat == 0:
                halo_copy(turn, move).wait()
                at = LEFT - HALF if dlon > 0 else LEFT + BS
                for k in range(HALF):
                    field[pl.ds(HALF * WIDE + at + k, BS, stride=WIDE), :] = h_recv[
                        turn, move, k
                    ].astype(F32)
            else:
                @pl.when(has(dlat))
                def _(move=move):
                    halo_copy(turn, move).wait_send()

                @pl.when(has(-dlat))
                def _(move=move, dlat=dlat, dlon=dlon):
                    halo_copy(turn, move).wait_recv()
                    at = 0 if dlat > 0 else BS + HALF
                    if move < 4:
                        field3[at : at + HALF, LEFT : LEFT + BS, :] = h_recv[turn, move].astype(F32)
                    else:
                        got = c_recv[turn, move - 4].astype(F32)
                        if dlon > 0:
                            field3[at : at + HALF, 0:LEFT, :] = got[:, 8:16, :]
                        else:
                            field3[at : at + HALF, LEFT + BS : WIDE, :] = got[:, 0:8, :]

    def spread_pairs(field3, pairs):
        def one(r, carry):
            for b in range(KS):
                for h in range(2):
                    pairs[b, r, :, h * C : (h + 1) * C] = field3[
                        2 * r + h, pl.ds(LEFT - HALF + b, BS), :
                    ].astype(BF16)
            return carry
        lax.fori_loop(0, PAIRS, one, 0)

    def conv_chunk(pairs, weights, t):
        taps = [
            pairs[b, pl.ds(8 * t + q, 8)].reshape(8 * BS, 2 * C) for b in range(KS) for q in range(4)
        ]
        return mm(jnp.concatenate(taps, axis=1), weights[...])

    halo_send(0, padf, padf3)

    eye = lax.broadcasted_iota(jnp.int32, (C, C), 0) == lax.broadcasted_iota(jnp.int32, (C, C), 1)
    none = jnp.zeros((C, C), BF16)
    for weights, flip in ((w_fwd, False), (w_bwd, True)):
        for b in range(KS):
            taps = []
            for a in range(KS):
                row = kern[KS - 1 - a, KS - 1 - b] if flip else kern[a, b]
                taps.append(jnp.where(eye, row[None, :], 0.0).astype(BF16))
            taps = [none] + taps + [none]
            for q in range(4):
                at = (b * 4 + q) * 2 * C
                weights[at : at + C, 0:C] = taps[2 * q + 1]
                weights[at : at + C, C : 2 * C] = taps[2 * q]
                weights[at + C : at + 2 * C, 0:C] = taps[2 * q + 2]
                weights[at + C : at + 2 * C, C : 2 * C] = taps[2 * q + 1]

    acc_in[...] = jnp.zeros_like(acc_in)
    acc_out[...] = jnp.zeros_like(acc_out)
    vecs[...] = jnp.zeros_like(vecs)
    halo_wait(0, padf, padf3)
    spread_pairs(padf3, padp)

    def conv_piece(t, first, last):
        taps = [
            padp[b, pl.ds(8 * t + q, 8)].reshape(8 * BS, 2 * C)
            for b in range(first, last) for q in range(4)
        ]
        out = mm(jnp.concatenate(taps, axis=1), w_fwd[first * 8 * C : last * 8 * C, :])
        rows = pl.ds(pl.multiple_of(t * 512, 512), 512)
        convb[rows, :] = out if first == 0 else convb[rows, :] + out

    conv_piece(0, 0, KS)

    c1 = math.sqrt(2.0 / math.pi)
    c2 = c1 * 0.044715
    order = (0, 2, 4, 6, 1, 3, 5, 7)

    def cell_chunk(t, beside=(None, None)):
        two = convb[pl.ds(pl.multiple_of(t * 256, 256), 256), :]
        conv = jnp.concatenate([two[:, :C], two[:, C:]], axis=0) + bias[...]
        centred = conv - jnp.mean(conv, axis=-1, keepdims=True)
        inverse_std = lax.rsqrt(jnp.mean(centred * centred, axis=-1, keepdims=True) + 1e-06)
        scaled = centred * inverse_std
        normed = (scaled * gain[...] + shift[...]).astype(BF16)
        og = jnp.concatenate([cot[8 * t + i] * maskx[8 * t + i] for i in order], axis=0)
        normed_t = normed.T
        og_t = og.T
        ones = jnp.ones((16, 512), BF16)
        left = jnp.concatenate([normed_t, ones], axis=0)
        norm_grad = jnp.zeros((512, C), F32)
        for h in range(2):
            if beside[h] is not None:
                beside[h]()
            cols = slice(h * 256, (h + 1) * 256)
            v = mm(normed, w_in[:, cols]) + b_in[:, cols]
            act_grad = mm(og, w_out[cols, :], ((1,), (1,)))
            v2 = v * v
            t_half = 0.5 + 0.5 * jnp.tanh(v * (c1 + c2 * v2))
            act = v * t_half
            slope = t_half + act * (1.0 - t_half) * (2.0 * c1 + 6.0 * c2 * v2)
            hidden = (act_grad * slope).astype(BF16)
            acc_out[:, cols] += mm(og_t, act.astype(BF16))
            acc_in[:, cols] += mm(left, hidden)
            norm_grad += mm(hidden, w_in[:, cols], ((1,), (1,)))
        weighted = norm_grad * gain[...]
        product = norm_grad * scaled
        g = inverse_std * (
            weighted
            - jnp.mean(weighted, axis=-1, keepdims=True)
            - scaled * jnp.mean(weighted * scaled, axis=-1, keepdims=True)
        )
        g = g.astype(BF16)
        wide = g.astype(F32)
        vecs[0] += wide.reshape(64, 8, C).sum(0)
        vecs[1] += product.reshape(64, 8, C).sum(0)
        vecs[2] += norm_grad.reshape(64, 8, C).sum(0)
        grad_t[:, pl.ds(pl.multiple_of(t * 256, 256), 256)] = jnp.concatenate(
            [g[:256], g[256:]], axis=1
        ).T
        for n, i in enumerate(order):
            gradf3[HALF + 8 * t + i, LEFT : LEFT + BS, :] = wide[n * BS : (n + 1) * BS]

    def two_chunks(t, carry):
        piece = functools.partial(conv_piece, t + 1)
        cell_chunk(2 * t, (lambda: piece(0, 2), lambda: piece(2, 4)))
        cell_chunk(2 * t + 1, (lambda: piece(4, 6), lambda: piece(6, 7)))
        return carry
    lax.fori_loop(0, 3, two_chunks, 0)

    def last_chunk(t, carry):
        cell_chunk(t)
        return carry
    lax.fori_loop(6, 8, last_chunk, 0)

    halo_send(1, gradf, gradf3)

    if big.shape[0] > BIG:
        big[BIG:, :] = jnp.zeros((big.shape[0] - BIG, C), F32)
    for h in range(4):
        big[h * C : (h + 1) * C, :] = acc_in[0:C, h * C : (h + 1) * C]
        big[HID + h * C : HID + (h + 1) * C, :] = acc_out[:, h * C : (h + 1) * C].T

    def copy(src, dst, group, mine, other, to):
        return pltpu.make_async_remote_copy(
            src_ref=src, dst_ref=dst.at[mine], send_sem=s_sem.at[group, other],
            recv_sem=r_sem.at[group, mine], device_id=to, device_id_type=MESH,
        )

    def arrived(dst, group, other, to):
        pltpu.make_async_remote_copy(
            src_ref=dst.at[other], dst_ref=dst.at[other], send_sem=s_sem.at[group, other],
            recv_sem=r_sem.at[group, other], device_id=to, device_id_type=MESH,
        ).wait_recv()

    def send_parts(src, rows, dst, group):
        for other in lons:
            at = pl.multiple_of(other * rows, 8)
            copy(src.at[pl.ds(at, rows)], dst, group, lon, other, dev(lat, other)).start()
        dst[lon] = src[pl.ds(pl.multiple_of(lon * rows, 8), rows), :]

    def end(src, rows, dst, group, peers, along):
        for other in peers:
            to = dev(lat, other) if along == "lon" else dev(other, lon)
            mine = lon if along == "lon" else lat
            copy(src.at[pl.ds(0, rows)], dst, group, mine, other, to).wait_send()
            arrived(dst, group, other, to)

    def total(slots, count):
        out = slots[0]
        for k in range(1, count):
            out = out + slots[k]
        return out

    send_parts(big, strip, big_lon, 0)

    def kernel_column(b, carry):
        rows = [jnp.zeros((1, C), F32) for _ in range(KS + 2)]
        for q in range(4):
            both = mm(grad_t[...], padp[b, q : q + 32].reshape(2048, 2 * C))

            def diagonal(e, s):
                block = both[e * C : (e + 1) * C, s * C : (s + 1) * C]
                return jnp.sum(jnp.where(eye, block, 0.0), axis=0, keepdims=True)
            rows[2 * q + 1] = rows[2 * q + 1] + diagonal(0, 0) + diagonal(1, 1)
            if q < 3:
                rows[2 * q + 2] = rows[2 * q + 2] + diagonal(0, 1)
            if q > 0:
                rows[2 * q] = rows[2 * q] + diagonal(1, 0)
        small[pl.ds(pl.multiple_of(b * 8, 8), 8), :] = jnp.concatenate(
            rows[1:8] + [jnp.zeros((1, C), F32)], axis=0
        )
        return carry
    lax.fori_loop(0, KS, kernel_column, 0)

    if small.shape[0] > SMALL:
        small[SMALL:, :] = jnp.zeros((small.shape[0] - SMALL, C), F32)
    small[56:64, :] = jnp.concatenate(
        [jnp.sum(vecs[k], axis=0, keepdims=True) for k in range(3)]
        + [acc_in[C : C + 1, h * C : (h + 1) * C] for h in range(4)]
        + [jnp.zeros((1, C), F32)],
        axis=0,
    )
    send_parts(small, small_part, small_lon, 1)

    end(big, strip, big_lon, 0, lons, "lon")
    big_sum[...] = total(big_lon, n_lon)
    for other in lats:
        at = pl.multiple_of(other * part, 8)
        copy(big_sum.at[pl.ds(at, part)], big_lat, 2, lat, other, dev(other, lon)).start()
    big_lat[lat] = big_sum[pl.ds(pl.multiple_of(lat * part, 8), part), :]

    halo_wait(1, gradf, gradf3)
    spread_pairs(gradf3, gradp)

    def backward(t):
        two = conv_chunk(gradp, w_bwd, t)
        for i in range(8):
            for e in range(2):
                row = 16 * t + 2 * i + e
                back = two[i * BS : (i + 1) * BS, e * C : (e + 1) * C]
                o_cells[row] = ((cot[row].astype(F32) + back) * maskx[row].astype(F32)).astype(BF16)

    factor = 1.0 / math.sqrt(float(BS * BS * n_lon * n_lat))
    own = pl.ds(pl.multiple_of(lat * part, 8), part)

    def spread_lat(other):
        return pltpu.make_async_remote_copy(
            src_ref=big_all.at[lon, own], dst_ref=big_all.at[lon, own],
            send_sem=s_sem.at[4, other], recv_sem=r_sem.at[4, lat],
            device_id=dev(other, lon), device_id_type=MESH,
        )

    end(big_sum, part, big_lat, 2, lats, "lat")
    big_all[lon, own, :] = total(big_lat, n_lat) * factor
    for other in lats:
        spread_lat(other).start()
    end(small, small_part, small_lon, 1, lons, "lon")
    small_sum[...] = total(small_lon, n_lon)
    for other in lats:
        copy(small_sum, small_lat, 3, lat, other, dev(other, lon)).start()
    small_lat[lat] = small_sum[...]

    backward(0)
    for other in lats:
        spread_lat(other).wait_send()
        theirs = big_all.at[lon, pl.ds(pl.multiple_of(other * part, 8), part)]
        pltpu.make_async_remote_copy(
            src_ref=theirs, dst_ref=theirs, send_sem=s_sem.at[4, other],
            recv_sem=r_sem.at[4, other], device_id=dev(other, lon), device_id_type=MESH,
        ).wait_recv()
    for other in lons:
        copy(big_all.at[lon], big_all, 5, lon, other, dev(lat, other)).start()
    end(small_sum, small_part, small_lat, 3, lats, "lat")
    small_all[lon] = total(small_lat, n_lat) * factor
    for other in lons:
        copy(small_all.at[lon], small_all, 6, lon, other, dev(lat, other)).start()

    backward(1)
    backward(2)
    backward(3)
    for other in lons:
        copy(big_all.at[lon], big_all, 5, lon, other, dev(lat, other)).wait_send()
        arrived(big_all, 5, other, dev(lat, other))
        copy(small_all.at[lon], small_all, 6, lon, other, dev(lat, other)).wait_send()
        arrived(small_all, 6, other, dev(lat, other))

    flat = big_all.reshape(n_lon * strip, C)
    for h in range(4):
        o_in[:, h * C : (h + 1) * C] = flat[h * C : (h + 1) * C, :]
    o_out[...] = flat[HID : 2 * HID, :]
    rest = small_all.reshape(n_lon * small_part, C)
    for a in range(KS):
        for b in range(KS):
            o_kernel[a, b : b + 1, :] = rest[8 * b + a : 8 * b + a + 1, :]
    o_bias[...] = rest[56:57, :]
    o_gain[...] = rest[57:58, :]
    o_shift[...] = rest[58:59, :]
    for h in range(4):
        o_b[:, h * C : (h + 1) * C] = rest[59 + h : 60 + h, :]


def hand_out(*refs):
    copies = [pltpu.make_async_copy(refs[k], refs[8 + k], refs[16].at[k]) for k in range(8)]
    for each in copies:
        each.start()
    for each in copies:
        each.wait()


def body(n_lon, n_lat, cells, ocean_mask, cotangent, kernel, conv_bias, gain, shift, w_in, b_in, w_out):
    part, small_part = plan(n_lon, n_lat)
    strip = n_lat * part
    vmem = pl.BlockSpec(memory_space=pltpu.VMEM)
    most = max(n_lon, n_lat)
    outs = pl.pallas_call(
        functools.partial(block_kernel, n_lon, n_lat),
        out_shape=(
            jax.ShapeDtypeStruct((BS, BS, C), BF16),
            jax.ShapeDtypeStruct((KS, KS, C), F32),
            jax.ShapeDtypeStruct((1, C), F32),
            jax.ShapeDtypeStruct((1, C), F32),
            jax.ShapeDtypeStruct((1, C), F32),
            jax.ShapeDtypeStruct((C, HID), F32),
            jax.ShapeDtypeStruct((1, HID), F32),
            jax.ShapeDtypeStruct((HID, C), F32),
        ),
        in_specs=[vmem] * 10,
        out_specs=(vmem,) * 8,
        scratch_shapes=[
            pltpu.VMEM((TALL * WIDE, C), F32),
            pltpu.VMEM((TALL * WIDE, C), F32),
            pltpu.VMEM((KS, PAIRS, BS, 2 * C), BF16),
            pltpu.VMEM((KS, PAIRS, BS, 2 * C), BF16),
            pltpu.VMEM((KS * 4 * 2 * C, 2 * C), BF16),
            pltpu.VMEM((KS * 4 * 2 * C, 2 * C), BF16),
            pltpu.VMEM((2048, 2 * C), F32),
            pltpu.VMEM((2 * C, 2048), BF16),
            pltpu.VMEM((BS, BS, C), BF16),
            pltpu.VMEM((C + 16, HID), F32),
            pltpu.VMEM((C, HID), F32),
            pltpu.VMEM((3, 8, C), F32),
            pltpu.VMEM((2, 4, HALF, BS, C), BF16),
            pltpu.VMEM((2, 4, HALF, BS, C), BF16),
            pltpu.VMEM((2, 4, HALF, 16, C), BF16),
            pltpu.VMEM((n_lon * strip, C), F32),
            pltpu.VMEM((n_lon, strip, C), F32),
            pltpu.VMEM((n_lat, part, C), F32),
            pltpu.VMEM((strip, C), F32),
            pltpu.VMEM((n_lon, strip, C), F32),
            pltpu.VMEM((n_lon * small_part, C), F32),
            pltpu.VMEM((n_lon, small_part, C), F32),
            pltpu.VMEM((n_lat, small_part, C), F32),
            pltpu.VMEM((small_part, C), F32),
            pltpu.VMEM((n_lon, small_part, C), F32),
            pltpu.SemaphoreType.DMA((2, 8)),
            pltpu.SemaphoreType.DMA((2, 8)),
            pltpu.SemaphoreType.DMA((7, most)),
            pltpu.SemaphoreType.DMA((7, most)),
        ],
        compiler_params=pltpu.CompilerParams(
            collective_id=0, has_side_effects=True, vmem_limit_bytes=56 * 2**20
        ),
    )(
        cells, ocean_mask, cotangent, kernel, conv_bias[None, :], gain[None, :], shift[None, :],
        w_in, b_in[None, :], w_out,
    )
    anywhere = pl.BlockSpec(memory_space=pl.ANY)
    outs = pl.pallas_call(
        hand_out,
        out_shape=tuple(jax.ShapeDtypeStruct(x.shape, x.dtype) for x in outs),
        in_specs=[anywhere] * 8,
        out_specs=(anywhere,) * 8,
        scratch_shapes=[pltpu.SemaphoreType.DMA((8,))],
    )(*outs)
    g_cells, g_kernel, g_bias, g_gain, g_shift, g_in, g_b, g_out = outs
    return (g_cells, g_kernel, g_bias[0], g_gain[0], g_shift[0], g_in, g_b[0], g_out)


def solution(mesh):
    grid = P("lat", "lon", None)
    in_specs = (grid, P("lat", "lon"), grid) + (P(),) * 7
    out_specs = (grid,) + (P(),) * 7
    return jax.shard_map(
        functools.partial(body, mesh.shape["lon"], mesh.shape["lat"]),
        mesh=mesh, in_specs=in_specs, out_specs=out_specs, check_vma=False,
    )
```

```python
import functools
import math

import jax
import jax.numpy as jnp
from jax import lax
from jax.experimental import pallas as pl
from jax.experimental.pallas import tpu as pltpu
from jax.sharding import PartitionSpec as P

KS = 7
HALF = 3
BS = 64
C = 128
HID = 512
LEFT = 8
WIDE = 80
TALL = BS + 2 * HALF
PAIRS = TALL // 2
BIG = 2 * HID
SMALL = 64
MESH = pl.DeviceIdType.MESH
F32 = jnp.float32
BF16 = jnp.bfloat16
MOVES = ((0, 1), (0, -1), (1, 0), (-1, 0), (1, 1), (1, -1), (-1, 1), (-1, -1))


def mm(a, b, dims=((1,), (0,))):
    return lax.dot_general(a, b, (dims, ((), ())), preferred_element_type=F32)


def plan(n_lon, n_lat):
    part = -(-BIG // (n_lon * n_lat * 16)) * 16
    small = max(SMALL // n_lon, 8)
    return part, small


def block_kernel(
    n_lon, n_lat,
    cells, mask, cot, kern, bias, gain, shift, w_in, b_in, w_out,
    o_cells, o_kernel, o_bias, o_gain, o_shift, o_in, o_b, o_out,
    padf, gradf, padp, gradp, w_fwd, w_bwd, convb, grad_t, maskx, acc_in, acc_out, vecs,
    h_send, h_recv, c_recv,
    big, big_lon, big_lat, big_sum, big_all, small, small_lon, small_lat, small_sum, small_all,
    hs_sem, hr_sem, s_sem, r_sem,
):
    part, small_part = plan(n_lon, n_lat)
    strip = n_lat * part
    lon = lax.axis_index("lon")
    lat = lax.axis_index("lat")
    lons = [lax.rem(lon + d, n_lon) for d in range(1, n_lon)]
    lats = [lax.rem(lat + d, n_lat) for d in range(1, n_lat)]

    def dev(a, b):
        return {"lat": a, "lon": b}

    def step_lon(d):
        return lax.rem(lon + d + n_lon, n_lon)

    def has(d):
        return (lat > 0) if d < 0 else (lat < n_lat - 1)

    barrier = pltpu.get_barrier_semaphore()
    for other in lons:
        pl.semaphore_signal(barrier, inc=1, device_id=dev(lat, other), device_id_type=MESH)
    for other in lats:
        pl.semaphore_signal(barrier, inc=1, device_id=dev(other, lon), device_id_type=MESH)
    for dlat, dlon in MOVES[4:]:
        corner = dev(lax.rem(lat + dlat + n_lat, n_lat), step_lon(dlon))
        pl.semaphore_signal(barrier, inc=1, device_id=corner, device_id_type=MESH)

    mask_t = mask[...].astype(F32).T
    padf3 = padf.reshape(TALL, WIDE, C)
    gradf3 = gradf.reshape(TALL, WIDE, C)
    for field in (padf3, gradf3):
        field[0:HALF] = jnp.zeros((HALF, WIDE, C), F32)
        field[BS + HALF : TALL] = jnp.zeros((HALF, WIDE, C), F32)
    for row in range(BS):
        spread = jnp.broadcast_to(mask_t[:, row : row + 1], (BS, C))
        maskx[row] = spread.astype(BF16)
        padf3[HALF + row, LEFT : LEFT + BS, :] = cells[row].astype(F32) * spread

    pl.semaphore_wait(barrier, n_lon + n_lat + 2)

    def halo_copy(turn, move):
        dlat, dlon = MOVES[move]
        if move < 4:
            src, dst = h_send.at[turn, move], h_recv.at[turn, move]
        else:
            src = h_send.at[turn, 2 if dlat > 0 else 3, :, pl.ds(48 if dlon > 0 else 0, 16), :]
            dst = c_recv.at[turn, move - 4]
        return pltpu.make_async_remote_copy(
            src_ref=src, dst_ref=dst,
            send_sem=hs_sem.at[turn, move], recv_sem=hr_sem.at[turn, move],
            device_id=dev(lat + dlat, step_lon(dlon)), device_id_type=MESH,
        )

    def halo_send(turn, field, field3):
        for k in range(HALF):
            last = field[pl.ds(HALF * WIDE + LEFT + BS - HALF + k, BS, stride=WIDE), :]
            first = field[pl.ds(HALF * WIDE + LEFT + k, BS, stride=WIDE), :]
            h_send[turn, 0, k] = last.astype(BF16)
            h_send[turn, 1, k] = first.astype(BF16)
            h_send[turn, 2, k] = field3[BS + k, LEFT : LEFT + BS, :].astype(BF16)
            h_send[turn, 3, k] = field3[HALF + k, LEFT : LEFT + BS, :].astype(BF16)
        for move, (dlat, _) in enumerate(MOVES):
            if dlat == 0:
                halo_copy(turn, move).start()
            else:
                @pl.when(has(dlat))
                def _(move=move):
                    halo_copy(turn, move).start()

    def halo_wait(turn, field, field3):
        for move, (dlat, dlon) in enumerate(MOVES):
            if dlat == 0:
                halo_copy(turn, move).wait()
                at = LEFT - HALF if dlon > 0 else LEFT + BS
                for k in range(HALF):
                    field[pl.ds(HALF * WIDE + at + k, BS, stride=WIDE), :] = h_recv[
                        turn, move, k
                    ].astype(F32)
            else:
                @pl.when(has(dlat))
                def _(move=move):
                    halo_copy(turn, move).wait_send()

                @pl.when(has(-dlat))
                def _(move=move, dlat=dlat, dlon=dlon):
                    halo_copy(turn, move).wait_recv()
                    at = 0 if dlat > 0 else BS + HALF
                    if move < 4:
                        field3[at : at + HALF, LEFT : LEFT + BS, :] = h_recv[turn, move].astype(F32)
                    else:
                        got = c_recv[turn, move - 4].astype(F32)
                        if dlon > 0:
                            field3[at : at + HALF, 0:LEFT, :] = got[:, 8:16, :]
                        else:
                            field3[at : at + HALF, LEFT + BS : WIDE, :] = got[:, 0:8, :]

    def spread_pairs(field3, pairs):
        def one(r, carry):
            for b in range(KS):
                for h in range(2):
                    pairs[b, r, :, h * C : (h + 1) * C] = field3[
                        2 * r + h, pl.ds(LEFT - HALF + b, BS), :
                    ].astype(BF16)
            return carry
        lax.fori_loop(0, PAIRS, one, 0)

    def conv_chunk(pairs, weights, t):
        taps = [
            pairs[b, pl.ds(8 * t + q, 8)].reshape(8 * BS, 2 * C) for b in range(KS) for q in range(4)
        ]
        return mm(jnp.concatenate(taps, axis=1), weights[...])

    halo_send(0, padf, padf3)

    eye = lax.broadcasted_iota(jnp.int32, (C, C), 0) == lax.broadcasted_iota(jnp.int32, (C, C), 1)
    none = jnp.zeros((C, C), BF16)
    for weights, flip in ((w_fwd, False), (w_bwd, True)):
        for b in range(KS):
            taps = []
            for a in range(KS):
                row = kern[KS - 1 - a, KS - 1 - b] if flip else kern[a, b]
                taps.append(jnp.where(eye, row[None, :], 0.0).astype(BF16))
            taps = [none] + taps + [none]
            for q in range(4):
                at = (b * 4 + q) * 2 * C
                weights[at : at + C, 0:C] = taps[2 * q + 1]
                weights[at : at + C, C : 2 * C] = taps[2 * q]
                weights[at + C : at + 2 * C, 0:C] = taps[2 * q + 2]
                weights[at + C : at + 2 * C, C : 2 * C] = taps[2 * q + 1]

    acc_in[...] = jnp.zeros_like(acc_in)
    acc_out[...] = jnp.zeros_like(acc_out)
    vecs[...] = jnp.zeros_like(vecs)
    halo_wait(0, padf, padf3)
    spread_pairs(padf3, padp)

    def conv_piece(t, first, last):
        taps = [
            padp[b, pl.ds(8 * t + q, 8)].reshape(8 * BS, 2 * C)
            for b in range(first, last) for q in range(4)
        ]
        out = mm(jnp.concatenate(taps, axis=1), w_fwd[first * 8 * C : last * 8 * C, :])
        rows = pl.ds(pl.multiple_of(t * 512, 512), 512)
        convb[rows, :] = out if first == 0 else convb[rows, :] + out

    conv_piece(0, 0, KS)

    c1 = math.sqrt(2.0 / math.pi)
    c2 = c1 * 0.044715
    order = (0, 2, 4, 6, 1, 3, 5, 7)

    def cell_chunk(t, beside=(None, None)):
        two = convb[pl.ds(pl.multiple_of(t * 256, 256), 256), :]
        conv = jnp.concatenate([two[:, :C], two[:, C:]], axis=0) + bias[...]
        centred = conv - jnp.mean(conv, axis=-1, keepdims=True)
        inverse_std = lax.rsqrt(jnp.mean(centred * centred, axis=-1, keepdims=True) + 1e-06)
        scaled = centred * inverse_std
        normed = (scaled * gain[...] + shift[...]).astype(BF16)
        og = jnp.concatenate([cot[8 * t + i] * maskx[8 * t + i] for i in order], axis=0)
        normed_t = normed.T
        og_t = og.T
        ones = jnp.ones((16, 512), BF16)
        left = jnp.concatenate([normed_t, ones], axis=0)
        norm_grad = jnp.zeros((512, C), F32)
        for h in range(2):
            if beside[h] is not None:
                beside[h]()
            cols = slice(h * 256, (h + 1) * 256)
            v = mm(normed, w_in[:, cols]) + b_in[:, cols]
            act_grad = mm(og, w_out[cols, :], ((1,), (1,)))
            v2 = v * v
            t_half = 0.5 + 0.5 * jnp.tanh(v * (c1 + c2 * v2))
            act = v * t_half
            slope = t_half + act * (1.0 - t_half) * (2.0 * c1 + 6.0 * c2 * v2)
            hidden = (act_grad * slope).astype(BF16)
            acc_out[:, cols] += mm(og_t, act.astype(BF16))
            acc_in[:, cols] += mm(left, hidden)
            norm_grad += mm(hidden, w_in[:, cols], ((1,), (1,)))
        weighted = norm_grad * gain[...]
        product = norm_grad * scaled
        g = inverse_std * (
            weighted
            - jnp.mean(weighted, axis=-1, keepdims=True)
            - scaled * jnp.mean(weighted * scaled, axis=-1, keepdims=True)
        )
        g = g.astype(BF16)
        wide = g.astype(F32)
        vecs[0] += wide.reshape(64, 8, C).sum(0)
        vecs[1] += product.reshape(64, 8, C).sum(0)
        vecs[2] += norm_grad.reshape(64, 8, C).sum(0)
        grad_t[:, pl.ds(pl.multiple_of(t * 256, 256), 256)] = jnp.concatenate(
            [g[:256], g[256:]], axis=1
        ).T
        for n, i in enumerate(order):
            gradf3[HALF + 8 * t + i, LEFT : LEFT + BS, :] = wide[n * BS : (n + 1) * BS]

    def two_chunks(t, carry):
        piece = functools.partial(conv_piece, t + 1)
        cell_chunk(2 * t, (lambda: piece(0, 2), lambda: piece(2, 4)))
        cell_chunk(2 * t + 1, (lambda: piece(4, 6), lambda: piece(6, 7)))
        return carry
    lax.fori_loop(0, 3, two_chunks, 0)

    def last_chunk(t, carry):
        cell_chunk(t)
        return carry
    lax.fori_loop(6, 8, last_chunk, 0)

    halo_send(1, gradf, gradf3)

    if big.shape[0] > BIG:
        big[BIG:, :] = jnp.zeros((big.shape[0] - BIG, C), F32)
    for h in range(4):
        big[h * C : (h + 1) * C, :] = acc_in[0:C, h * C : (h + 1) * C]
        big[HID + h * C : HID + (h + 1) * C, :] = acc_out[:, h * C : (h + 1) * C].T

    def copy(src, dst, group, mine, other, to):
        return pltpu.make_async_remote_copy(
            src_ref=src, dst_ref=dst.at[mine], send_sem=s_sem.at[group, other],
            recv_sem=r_sem.at[group, mine], device_id=to, device_id_type=MESH,
        )

    def arrived(dst, group, other, to):
        pltpu.make_async_remote_copy(
            src_ref=dst.at[other], dst_ref=dst.at[other], send_sem=s_sem.at[group, other],
            recv_sem=r_sem.at[group, other], device_id=to, device_id_type=MESH,
        ).wait_recv()

    def send_parts(src, rows, dst, group):
        for other in lons:
            at = pl.multiple_of(other * rows, 8)
            copy(src.at[pl.ds(at, rows)], dst, group, lon, other, dev(lat, other)).start()
        dst[lon] = src[pl.ds(pl.multiple_of(lon * rows, 8), rows), :]

    def end(src, rows, dst, group, peers, along):
        for other in peers:
            to = dev(lat, other) if along == "lon" else dev(other, lon)
            mine = lon if along == "lon" else lat
            copy(src.at[pl.ds(0, rows)], dst, group, mine, other, to).wait_send()
            arrived(dst, group, other, to)

    def total(slots, count):
        out = slots[0]
        for k in range(1, count):
            out = out + slots[k]
        return out

    send_parts(big, strip, big_lon, 0)

    def kernel_column(b, carry):
        rows = [jnp.zeros((1, C), F32) for _ in range(KS + 2)]
        for q in range(4):
            both = mm(grad_t[...], padp[b, q : q + 32].reshape(2048, 2 * C))

            def diagonal(e, s):
                block = both[e * C : (e + 1) * C, s * C : (s + 1) * C]
                return jnp.sum(jnp.where(eye, block, 0.0), axis=0, keepdims=True)
            rows[2 * q + 1] = rows[2 * q + 1] + diagonal(0, 0) + diagonal(1, 1)
            if q < 3:
                rows[2 * q + 2] = rows[2 * q + 2] + diagonal(0, 1)
            if q > 0:
                rows[2 * q] = rows[2 * q] + diagonal(1, 0)
        small[pl.ds(pl.multiple_of(b * 8, 8), 8), :] = jnp.concatenate(
            rows[1:8] + [jnp.zeros((1, C), F32)], axis=0
        )
        return carry
    lax.fori_loop(0, KS, kernel_column, 0)

    if small.shape[0] > SMALL:
        small[SMALL:, :] = jnp.zeros((small.shape[0] - SMALL, C), F32)
    small[56:64, :] = jnp.concatenate(
        [jnp.sum(vecs[k], axis=0, keepdims=True) for k in range(3)]
        + [acc_in[C : C + 1, h * C : (h + 1) * C] for h in range(4)]
        + [jnp.zeros((1, C), F32)],
        axis=0,
    )
    send_parts(small, small_part, small_lon, 1)

    end(big, strip, big_lon, 0, lons, "lon")
    big_sum[...] = total(big_lon, n_lon)
    for other in lats:
        at = pl.multiple_of(other * part, 8)
        copy(big_sum.at[pl.ds(at, part)], big_lat, 2, lat, other, dev(other, lon)).start()
    big_lat[lat] = big_sum[pl.ds(pl.multiple_of(lat * part, 8), part), :]

    halo_wait(1, gradf, gradf3)
    spread_pairs(gradf3, gradp)

    def backward(t):
        two = conv_chunk(gradp, w_bwd, t)
        for i in range(8):
            for e in range(2):
                row = 16 * t + 2 * i + e
                back = two[i * BS : (i + 1) * BS, e * C : (e + 1) * C]
                o_cells[row] = ((cot[row].astype(F32) + back) * maskx[row].astype(F32)).astype(BF16)

    factor = 1.0 / math.sqrt(float(BS * BS * n_lon * n_lat))
    own = pl.ds(pl.multiple_of(lat * part, 8), part)

    def spread_lat(other):
        return pltpu.make_async_remote_copy(
            src_ref=big_all.at[lon, own], dst_ref=big_all.at[lon, own],
            send_sem=s_sem.at[4, other], recv_sem=r_sem.at[4, lat],
            device_id=dev(other, lon), device_id_type=MESH,
        )

    end(big_sum, part, big_lat, 2, lats, "lat")
    big_all[lon, own, :] = total(big_lat, n_lat) * factor
    for other in lats:
        spread_lat(other).start()
    end(small, small_part, small_lon, 1, lons, "lon")
    small_sum[...] = total(small_lon, n_lon)
    for other in lats:
        copy(small_sum, small_lat, 3, lat, other, dev(other, lon)).start()
    small_lat[lat] = small_sum[...]

    backward(0)
    for other in lats:
        spread_lat(other).wait_send()
        theirs = big_all.at[lon, pl.ds(pl.multiple_of(other * part, 8), part)]
        pltpu.make_async_remote_copy(
            src_ref=theirs, dst_ref=theirs, send_sem=s_sem.at[4, other],
            recv_sem=r_sem.at[4, other], device_id=dev(other, lon), device_id_type=MESH,
        ).wait_recv()
    for other in lons:
        copy(big_all.at[lon], big_all, 5, lon, other, dev(lat, other)).start()
    end(small_sum, small_part, small_lat, 3, lats, "lat")
    small_all[lon] = total(small_lat, n_lat) * factor
    for other in lons:
        copy(small_all.at[lon], small_all, 6, lon, other, dev(lat, other)).start()

    backward(1)
    backward(2)
    backward(3)
    for other in lons:
        copy(big_all.at[lon], big_all, 5, lon, other, dev(lat, other)).wait_send()
        arrived(big_all, 5, other, dev(lat, other))
        copy(small_all.at[lon], small_all, 6, lon, other, dev(lat, other)).wait_send()
        arrived(small_all, 6, other, dev(lat, other))

    flat = big_all.reshape(n_lon * strip, C)
    for h in range(4):
        o_in[:, h * C : (h + 1) * C] = flat[h * C : (h + 1) * C, :]
    o_out[...] = flat[HID : 2 * HID, :]
    rest = small_all.reshape(n_lon * small_part, C)
    for a in range(KS):
        for b in range(KS):
            o_kernel[a, b : b + 1, :] = rest[8 * b + a : 8 * b + a + 1, :]
    o_bias[...] = rest[56:57, :]
    o_gain[...] = rest[57:58, :]
    o_shift[...] = rest[58:59, :]
    for h in range(4):
        o_b[:, h * C : (h + 1) * C] = rest[59 + h : 60 + h, :]


def hand_out(*refs):
    for k in range(8):
        refs[8 + k][...] = refs[k][...]


def body(n_lon, n_lat, cells, ocean_mask, cotangent, kernel, conv_bias, gain, shift, w_in, b_in, w_out):
    part, small_part = plan(n_lon, n_lat)
    strip = n_lat * part
    vmem = pl.BlockSpec(memory_space=pltpu.VMEM)
    most = max(n_lon, n_lat)
    outs = pl.pallas_call(
        functools.partial(block_kernel, n_lon, n_lat),
        out_shape=(
            jax.ShapeDtypeStruct((BS, BS, C), BF16),
            jax.ShapeDtypeStruct((KS, KS, C), F32),
            jax.ShapeDtypeStruct((1, C), F32),
            jax.ShapeDtypeStruct((1, C), F32),
            jax.ShapeDtypeStruct((1, C), F32),
            jax.ShapeDtypeStruct((C, HID), F32),
            jax.ShapeDtypeStruct((1, HID), F32),
            jax.ShapeDtypeStruct((HID, C), F32),
        ),
        in_specs=[vmem] * 10,
        out_specs=(vmem,) * 8,
        scratch_shapes=[
            pltpu.VMEM((TALL * WIDE, C), F32),
            pltpu.VMEM((TALL * WIDE, C), F32),
            pltpu.VMEM((KS, PAIRS, BS, 2 * C), BF16),
            pltpu.VMEM((KS, PAIRS, BS, 2 * C), BF16),
            pltpu.VMEM((KS * 4 * 2 * C, 2 * C), BF16),
            pltpu.VMEM((KS * 4 * 2 * C, 2 * C), BF16),
            pltpu.VMEM((2048, 2 * C), F32),
            pltpu.VMEM((2 * C, 2048), BF16),
            pltpu.VMEM((BS, BS, C), BF16),
            pltpu.VMEM((C + 16, HID), F32),
            pltpu.VMEM((C, HID), F32),
            pltpu.VMEM((3, 8, C), F32),
            pltpu.VMEM((2, 4, HALF, BS, C), BF16),
            pltpu.VMEM((2, 4, HALF, BS, C), BF16),
            pltpu.VMEM((2, 4, HALF, 16, C), BF16),
            pltpu.VMEM((n_lon * strip, C), F32),
            pltpu.VMEM((n_lon, strip, C), F32),
            pltpu.VMEM((n_lat, part, C), F32),
            pltpu.VMEM((strip, C), F32),
            pltpu.VMEM((n_lon, strip, C), F32),
            pltpu.VMEM((n_lon * small_part, C), F32),
            pltpu.VMEM((n_lon, small_part, C), F32),
            pltpu.VMEM((n_lat, small_part, C), F32),
            pltpu.VMEM((small_part, C), F32),
            pltpu.VMEM((n_lon, small_part, C), F32),
            pltpu.SemaphoreType.DMA((2, 8)),
            pltpu.SemaphoreType.DMA((2, 8)),
            pltpu.SemaphoreType.DMA((7, most)),
            pltpu.SemaphoreType.DMA((7, most)),
        ],
        compiler_params=pltpu.CompilerParams(
            collective_id=0, has_side_effects=True, vmem_limit_bytes=56 * 2**20
        ),
    )(
        cells, ocean_mask, cotangent, kernel, conv_bias[None, :], gain[None, :], shift[None, :],
        w_in, b_in[None, :], w_out,
    )
    outs = pl.pallas_call(
        hand_out,
        out_shape=tuple(jax.ShapeDtypeStruct(x.shape, x.dtype) for x in outs),
        in_specs=[vmem] * 8,
        out_specs=(vmem,) * 8,
    )(*outs)
    g_cells, g_kernel, g_bias, g_gain, g_shift, g_in, g_b, g_out = outs
    return (g_cells, g_kernel, g_bias[0], g_gain[0], g_shift[0], g_in, g_b[0], g_out)


def solution(mesh):
    grid = P("lat", "lon", None)
    in_specs = (grid, P("lat", "lon"), grid) + (P(),) * 7
    out_specs = (grid,) + (P(),) * 7
    return jax.shard_map(
        functools.partial(body, mesh.shape["lon"], mesh.shape["lat"]),
        mesh=mesh, in_specs=in_specs, out_specs=out_specs, check_vma=False,
    )
```
